512 devices in a mesh: rep: 2 (over core), vocab: 64 (over z, x), tok: 4 (over y).
Axes of the slice: x: 4, y: 4, z: 16, core: 2. Of those that a mesh axis runs over, the one named last changes fastest.
Arguments:
- hidden: bfloat16 [2, 384, 3072], P('rep', None, 'tok'), may hold values from -48 to 48
- head_weight: bfloat16 [2, 3072, 81920], P('rep', 'tok', 'vocab'), may hold values from -0.5 to 0.5
- token_ids: int32 [384], replicated, may hold values from 0 to 81919
Outputs:
- per_token_loss: float32 [2, 384], P('rep', 'tok')
- weight_grad: bfloat16 [2, 3072, 81920], P('rep', 'tok', 'vocab')
- hidden_grad: bfloat16 [2, 384, 3072], P('rep', 'vocab', 'tok')
The draws below stay inside these ranges and needn't reach their ends.
All inputs are finite; a program needn't handle non-finite values.
Results may differ from the reference program's by a relative error of at most 0.0041.
Values may be sent and summed in bfloat16 or wider, within the bound.
A program may use at most 64 MiB of HBM per device.

```python
import math
import jax
import jax.numpy as jnp
import numpy as np
from jax import lax

D = 3072
TOKENS = 384
VOCAB = 81920


def draw_hidden(key, part):
    key = jax.random.fold_in(key, 11)
    key_normal = jax.random.fold_in(key, 0)
    normal_part = jax.random.normal(key_normal, (2, TOKENS, D), jnp.float32)
    values = jnp.clip(3.0 * normal_part, -24.0, 24.0)
    return values.astype(jnp.bfloat16)


def draw_head_weight(key, part):
    key = jax.random.fold_in(key, 23)
    key_normal = jax.random.fold_in(key, 0)
    inverse_root = 1.0 / math.sqrt(D)
    normal_part = jnp.clip(jax.random.normal(key_normal, (2, D, VOCAB), jnp.float32), -6.0, 6.0) * inverse_root
    column_rise = 0.9 + 0.2 * jnp.arange(VOCAB, dtype=jnp.float32) / VOCAB
    values = normal_part * column_rise
    return values.astype(jnp.bfloat16)


def touch_ends(entries, rng, least, top_value):
    spot = [jax.random.randint(jax.random.fold_in(rng, axis), (), 0, length) for axis, length in enumerate(entries.shape)]
    main_axis = entries.shape.index(max(entries.shape))
    beside = spot[:main_axis] + [(spot[main_axis] + 1) % entries.shape[main_axis]] + spot[main_axis + 1:]
    return entries.at[tuple(spot)].set(least).at[tuple(beside)].set(top_value)


def wide_ids(stream_key, shape, number_of, skew):
    loads = [min(1 << octave, number_of + 1 - (1 << octave)) * (1 << 20) // math.isqrt((1 << octave) ** skew) + 1 for octave in range((number_of + 1).bit_length()) if 1 << octave <= number_of]
    spread = 1 + sum(loads) // (1 << 30)
    table = np.cumsum(np.array([max(1, weight // spread) for weight in loads]))
    ticket = jax.random.randint(jax.random.fold_in(stream_key, 1), shape, 0, int(table[len(loads) - 1]))
    start = jnp.left_shift(1, jnp.searchsorted(jnp.asarray(table, jnp.int32), ticket, side="right").astype(jnp.int32))
    standing = start - 1 + jax.random.randint(jax.random.fold_in(stream_key, 4), shape, 0, 1 << 30) % jnp.minimum(start, number_of + 1 - start)
    return jax.random.permutation(jax.random.fold_in(stream_key, 2), number_of)[standing].astype(jnp.int32)


def setup_inputs(seed: int = 0) -> dict:
    key_list = jax.random.split(jax.random.key(seed), 4)
    return {
        "hidden": draw_hidden(jax.random.fold_in(key_list[3], 71), 0),
        "head_weight": draw_head_weight(jax.random.fold_in(key_list[3], 71), 0),
        "token_ids": touch_ends(wide_ids(key_list[2], (TOKENS,), VOCAB, 2), jax.random.fold_in(key_list[2], 3), 0, VOCAB - 1).astype(jnp.int32),
    }


smoothing_divisor = 2.0
mimicry_coefficient = 0.5


def replica_stats(score_matrix, token_ids):
    largest_entry_each = jnp.max(score_matrix, axis=1)
    centered_scores = score_matrix - largest_entry_each[:, None]
    norm_sum = jnp.sum(jnp.exp(centered_scores), axis=1)
    smoothed_accumulated = jnp.sum(jnp.exp(centered_scores / smoothing_divisor), axis=1)
    chosen_target_score = jnp.take_along_axis(score_matrix, token_ids[:, None].astype(jnp.int32), axis=1)[:, 0]
    normalizer_logarithm = largest_entry_each + jnp.log(norm_sum)
    smoothed_aggregate = largest_entry_each / smoothing_divisor + jnp.log(smoothed_accumulated)
    smoothed_logarithm = score_matrix / smoothing_divisor - smoothed_aggregate[:, None]
    return normalizer_logarithm, chosen_target_score, smoothed_logarithm


def reference(hidden, head_weight, token_ids):
    logits_pair = [jnp.dot(hidden[replica], head_weight[replica], preferred_element_type=jnp.float32) for replica in range(2)]
    stats_pair = [replica_stats(logits_pair[replica], token_ids) for replica in range(2)]
    vocab_ids = jnp.arange(VOCAB, dtype=jnp.int32)
    target_hit = vocab_ids[None, :] == token_ids[:, None].astype(jnp.int32)
    copy_objectives = []
    weight_grads = []
    hidden_grads = []
    for replica in range(2):
        score_matrix = logits_pair[replica]
        normalizer_logarithm, chosen_target_score, smoothed_logarithm = stats_pair[replica]
        teacher_log = stats_pair[1 - replica][2]
        guide_distribution = jnp.exp(teacher_log)
        relative_entropy_amount = jnp.sum(guide_distribution * (teacher_log - smoothed_logarithm), axis=1)
        copy_objectives.append(normalizer_logarithm - chosen_target_score + mimicry_coefficient * smoothing_divisor * smoothing_divisor * relative_entropy_amount)
        score_grad = (jnp.exp(score_matrix - normalizer_logarithm[:, None]) - target_hit.astype(jnp.float32)
                      + mimicry_coefficient * smoothing_divisor * (jnp.exp(smoothed_logarithm) - guide_distribution)).astype(jnp.bfloat16)
        weight_grads.append(lax.dot_general(hidden[replica], score_grad, (((0,), (0,)), ((), ())),
                                            preferred_element_type=jnp.float32).astype(jnp.bfloat16))
        hidden_grads.append(lax.dot_general(score_grad, head_weight[replica], (((1,), (1,)), ((), ())),
                                            preferred_element_type=jnp.float32).astype(jnp.bfloat16))
    return jnp.stack(copy_objectives), jnp.stack(weight_grads), jnp.stack(hidden_grads)
```

```python
import functools

import jax
import jax.numpy as jnp
from jax import lax
from jax.experimental import pallas as pl
from jax.experimental.pallas import tpu as pltpu
from jax.sharding import PartitionSpec as P

F32, BF16 = jnp.float32, jnp.bfloat16
NX, NZ, NY = 4, 16, 4
CHUNKS = 8
ROWS = 48
HALF = 640
MESH = pl.DeviceIdType.MESH


def rows_of(m):
    return pl.ds(pl.multiple_of(m * ROWS, 16), ROWS)


def dot(a, b, ca, cb):
    return lax.dot_general(a, b, (((ca,), (cb,)), ((), ())), preferred_element_type=F32)


def kernel(
    hid, wt, ids, loss_out, wg_out, hg_out,
    w_v, h_v, ht_v, acc, fbuf, cbuf, rx, pr, lg, sg, s1, hgs, xr, zs, zr, wg_v, xst, zst, lb,
    load_sem, out_sem, a_send, a_recv, st_send, st_recv, zst_send, zst_recv, l_send, l_recv,
    g_send, g_recv, x_send, x_recv, z_send, z_recv,
):
    c = lax.axis_index("rep")
    v = lax.axis_index("vocab")
    y = lax.axis_index("tok")
    z, x = v // NX, v % NX
    pc = 1 - c
    R, L, O = (y + 1) % NY, (y + 3) % NY, (y + 2) % NY
    mine = y + 4 * c
    cores = (c, pc)

    def xid(d):
        return {"vocab": z * NX + (x + d) % NX}

    def zid(zz):
        return {"vocab": zz * NX + x}

    def yid(core, yy):
        return {"rep": core, "tok": yy}

    loads = [
        pltpu.make_async_copy(hid.at[0], h_v, load_sem.at[0]),
        pltpu.make_async_copy(wt.at[0, :, pl.ds(0, HALF)], w_v.at[0], load_sem.at[1]),
        pltpu.make_async_copy(wt.at[0, :, pl.ds(HALF, HALF)], w_v.at[1], load_sem.at[2]),
    ]
    for cp in loads:
        cp.start()

    barrier = pltpu.get_barrier_semaphore()
    peers = [yid(cores[s], yy) for s in range(2) for yy in (y, R, L, O)][1:]
    peers += [xid(d) for d in range(1, NX)] + [zid((z + d) % NZ) for d in range(1, NZ)]
    for p in peers:
        pl.semaphore_signal(barrier, inc=1, device_id=p, device_id_type=MESH)

    def remote(src, dst, ss, rs, dev):
        return pltpu.make_async_remote_copy(
            src_ref=src, dst_ref=dst, send_sem=ss, recv_sem=rs, device_id=dev, device_id_type=MESH
        )

    sends = []

    def start(cp):
        cp.start()
        sends.append(cp)

    loads[0].wait()
    for a in range(2):
        loads[1 + a].wait()
        part = dot(h_v[...], w_v[a], 1, 0)
        acc[a] = part
        if a == 0:
            pl.semaphore_wait(barrier, len(peers))
        near, far = ((R, L), (L, R))[a]
        for s in range(2):
            i = 2 * a + s
            start(remote(acc.at[a, rows_of(O + 4 * cores[s])], fbuf.at[a, s],
                         a_send.at[i], a_recv.at[i], yid(c, near)))
        for s in range(2):
            i = 4 + 2 * a + s
            start(remote(acc.at[a, rows_of(far + 4 * cores[s])], rx.at[0, a, s],
                         a_send.at[i], a_recv.at[i], yid(cores[s], far)))
        start(remote(acc.at[a, rows_of(y + 4 * pc)], pr.at[a],
                     a_send.at[12 + a], a_recv.at[12 + a], yid(pc, y)))
    for s in range(2):
        for a in range(2):
            i = 2 * a + s
            near = (R, L)[a]
            m = rows_of(near + 4 * cores[s])
            remote(acc.at[a, m], fbuf.at[a, s], a_send.at[i], a_recv.at[i], yid(c, near)).wait_recv()
            cbuf[a, s] = acc[a, m] + fbuf[a, s]
            start(remote(cbuf.at[a, s], rx.at[1, a, s], a_send.at[8 + i], a_recv.at[8 + i],
                         yid(cores[s], near)))

    ht_v[...] = h_v[...].T
    spot = lax.broadcasted_iota(jnp.int32, (ROWS, 384), 1) - lax.broadcasted_iota(jnp.int32, (ROWS, 384), 0)
    id_col = jnp.sum(jnp.where(spot == mine * ROWS, ids[...], 0), axis=1, keepdims=True) - v * (2 * HALF)

    for a in range(2):
        remote(acc.at[a, rows_of(mine)], pr.at[a], a_send.at[12 + a], a_recv.at[12 + a], yid(pc, y)).wait_recv()
    for s in range(2):
        for a in range(2):
            for k in range(2):
                i = 4 + 4 * k + 2 * a + s
                remote(cbuf.at[a, s], rx.at[k, a, s], a_send.at[i], a_recv.at[i], yid(c, R)).wait_recv()
            own = acc[a, rows_of(mine)] if s == 0 else pr[a]
            lg[s, a] = own + rx[0, a, s] + rx[1, a, s]

    cols = lax.broadcasted_iota(jnp.int32, (ROWS, HALF), 1)
    lane = lax.broadcasted_iota(jnp.int32, (ROWS, 128), 1)
    tiles = []
    pad = jnp.zeros((16, 128), F32)
    for s in range(2):
        la, lbh = lg[s, 0], lg[s, 1]
        top = jnp.maximum(jnp.max(la, axis=1, keepdims=True), jnp.max(lbh, axis=1, keepdims=True))
        tot = [0.0] * 4
        for a, l in ((0, la), (1, lbh)):
            e = jnp.exp((l - top) * 0.5)
            hit = cols == id_col - a * HALF
            for n, term in enumerate((e * e, e, jnp.where(hit, l, 0.0), e * (0.5 * (l - lg[1 - s, a])))):
                tot[n] = tot[n] + jnp.sum(term, axis=1, keepdims=True)
        tile = jnp.where(lane == 0, top, 0.0)
        for n in range(4):
            tile = jnp.where(lane == n + 1, tot[n], tile)
        tiles += [tile, pad]
    stat = jnp.concatenate(tiles, axis=0).T[:8]

    def merge(parts):
        tops = functools.reduce(jnp.maximum, [p[0:1] for p in parts])
        total = [0.0] * 4
        for p in parts:
            f = jnp.exp((p[0:1] - tops) * 0.5)
            for n, w in enumerate((f * f, f, 1.0, f)):
                total[n] = total[n] + p[n + 1:n + 2] * w
        return tops, total

    xst[0] = stat
    for d in range(1, NX):
        start(remote(xst.at[0], xst.at[d], st_send.at[d], st_recv.at[d], xid(d)))
    for d in range(1, NX):
        remote(xst.at[0], xst.at[d], st_send.at[d], st_recv.at[d], xid(d)).wait_recv()
    tops, total = merge([xst[d] for d in range(NX)])
    zst[0] = jnp.concatenate([tops] + total + [jnp.zeros((3, 128), F32)], axis=0)
    for d in range(1, NZ):
        start(remote(zst.at[0], zst.at[d], zst_send.at[d], zst_recv.at[d], zid((z + d) % NZ)))
    for d in range(1, NZ):
        remote(zst.at[0], zst.at[d], zst_send.at[d], zst_recv.at[d], zid((z + d) % NZ)).wait_recv()
    tops, total = merge([zst[d] for d in range(NZ)])
    log_total = tops + jnp.log(total[0])
    tau_total = tops * 0.5 + jnp.log(total[1])
    ratio = pltpu.roll(total[3] / total[1] - tau_total, 64, 1) + tau_total
    loss = log_total - total[2] + 2.0 * ratio
    back = jnp.concatenate([log_total, tau_total, jnp.zeros((126, 128), F32)], axis=0).T

    mr = rows_of(mine)
    for a in range(2):
        hit = jnp.where(cols == id_col - a * HALF, 1.0, 0.0)
        l = [lg[0, a], lg[1, a]]
        q = [jnp.exp(l[s] * 0.5 - back[64 * s:64 * s + ROWS, 1:2]) for s in range(2)]
        for s in range(2):
            g = (jnp.exp(l[s] - back[64 * s:64 * s + ROWS, 0:1]) - hit + (q[s] - q[1 - s])).astype(BF16)
            if s == 0:
                sg[a, mr] = g
            else:
                s1[a] = g
        for s in range(2):
            src = sg.at[a, mr] if s == 0 else s1.at[a]
            i = 2 * a + s
            start(remote(src, sg.at[a, mr], g_send.at[i], g_recv.at[i], yid(cores[s], (R, L)[a])))
        start(remote(s1.at[a], sg.at[a, mr], g_send.at[12 + a], g_recv.at[12 + a], yid(pc, y)))
    for a in range(2):
        for s in range(2):
            src = sg.at[a, mr] if s == 0 else s1.at[a]
            i = 4 + 2 * a + s
            start(remote(src, sg.at[a, mr], g_send.at[i], g_recv.at[i], yid(cores[s], (L, R)[a])))

    lb[mine] = jnp.concatenate([loss, jnp.zeros((7, 128), F32)], axis=0)
    for e in range(1, CHUNKS):
        t = (mine + e) % CHUNKS
        start(remote(lb.at[mine], lb.at[mine], l_send.at[e], l_recv.at[mine], yid(t // 4, t % 4)))

    rr = lax.broadcasted_iota(jnp.int32, (64, ROWS), 0)
    tt = lax.broadcasted_iota(jnp.int32, (64, ROWS), 1)
    inner = rr % 8
    place = jnp.where((tt == (rr % 16) // 8 * 24 + rr // 16 * 6 + inner) & (inner < 6), 1.0, 0.0).astype(BF16)

    def hidden_part(k, m):
        r = rows_of(m)
        part = dot(sg[0, r], w_v[0], 1, 1) + dot(sg[1, r], w_v[1], 1, 1)
        hgs[k] = dot(place, part.astype(BF16), 1, 0).astype(BF16)
        for d in range(1, NX):
            xx = pl.multiple_of((x + d) % NX * 16, 16)
            start(remote(hgs.at[k, pl.ds(xx, 16)], xr.at[k, d], x_send.at[k, d], x_recv.at[k, d], xid(d)))

    def x_sum(k, m):
        total = hgs[k, pl.ds(pl.multiple_of(x * 16, 16), 16)].astype(F32)
        for d in range(1, NX):
            remote(hgs.at[k, pl.ds(0, 16)], xr.at[k, d], x_send.at[k, d], x_recv.at[k, d], xid(d)).wait_recv()
            total = total + xr[k, d].astype(F32)
        for i in range(2):
            t = total[8 * i:8 * i + 8]
            zs[k, i] = jnp.concatenate([t[:, :384], t[:, 384:]], axis=0).astype(BF16)
            zz = 2 * m + i
            d = (zz - z + NZ) % NZ

            @pl.when(d != 0)
            def _():
                remote(zs.at[k, i], zr.at[d], z_send.at[d], z_recv.at[d], zid(zz)).start()

            @pl.when(d == 0)
            def _():
                zr[0] = zs[k, i]

    def got(i, a, m, dev):
        remote(sg.at[a, rows_of(m)], sg.at[a, rows_of(m)], g_send.at[i], g_recv.at[i], dev).wait_recv()

    order = [mine, y + 4 * pc] + [n + 4 * cores[s] for s in range(2) for n in (L, R)]
    order += [O + 4 * cores[s] for s in range(2)]
    hidden_part(0, order[0])
    for a in range(2):
        got(12 + a, a, order[1], yid(pc, y))
    hidden_part(1, order[1])
    x_sum(0, order[0])
    for s in range(2):
        for a in range(2):
            m = (L, R)[a] + 4 * cores[s]
            got(2 * a + s, a, m, yid(c, L))
            start(remote(sg.at[a, rows_of(m)], sg.at[a, rows_of(m)], g_send.at[8 + 2 * a + s],
                         g_recv.at[8 + 2 * a + s], yid(c, (R, L)[a])))
    k = 2
    for s in range(2):
        for a in range(2):
            m = order[k]
            got(4 + 2 * (1 - a) + s, 1 - a, m, yid(c, L))
            hidden_part(k, m)
            x_sum(k - 1, order[k - 1])
            k += 1
    for s in range(2):
        for a in range(2):
            got(8 + 2 * a + s, a, order[k], yid(c, L))
        hidden_part(k, order[k])
        x_sum(k - 1, order[k - 1])
        k += 1

    outs = []
    for a in range(2):
        wg_v[a] = dot(ht_v[...], sg[a], 1, 0).astype(BF16)
        cp = pltpu.make_async_copy(wg_v.at[a], wg_out.at[0, :, pl.ds(a * HALF, HALF)], out_sem.at[a])
        cp.start()
        outs.append(cp)
        if a == 0:
            x_sum(k - 1, order[k - 1])

    for e in range(1, CHUNKS):
        t = (mine + e) % CHUNKS
        remote(lb.at[t], lb.at[t], l_send.at[e], l_recv.at[t], yid(pc, y)).wait_recv()
    pieces = []
    for i in range(2):
        m = 2 * y + i
        row = lb[m][0:1]
        pieces.append(jnp.where(m // 4 == c, row, pltpu.roll(row, 64, 1)))
    lanes = lax.broadcasted_iota(jnp.int32, (1, 128), 1)
    loss_out[...] = jnp.where(lanes < ROWS, pieces[0], pltpu.roll(pieces[1], ROWS, 1))[:, :96]

    for d in range(1, NZ):
        remote(zr.at[d], zr.at[d], z_send.at[d], z_recv.at[d], zid(z)).wait_recv()
    total = zr[0].astype(F32)
    for d in range(1, NZ):
        total = total + zr[d].astype(F32)
    hg_out[0] = jnp.concatenate([total[:8], total[8:]], axis=1)[:6].astype(BF16)

    for cp in sends:
        cp.wait_send()
    for d in range(1, NZ):
        remote(zr.at[d], zr.at[d], z_send.at[d], z_recv.at[d], zid((z + d) % NZ)).wait_send()
    for cp in outs:
        cp.wait()


def body(hidden, head_weight, token_ids):
    dma = pltpu.SemaphoreType.DMA
    return pl.pallas_call(
        kernel,
        out_shape=(
            jax.ShapeDtypeStruct((1, 96), F32),
            jax.ShapeDtypeStruct((1, 768, 2 * HALF), BF16),
            jax.ShapeDtypeStruct((1, 6, 768), BF16),
        ),
        in_specs=[
            pl.BlockSpec(memory_space=pl.ANY),
            pl.BlockSpec(memory_space=pl.ANY),
            pl.BlockSpec(memory_space=pltpu.VMEM),
        ],
        out_specs=(
            pl.BlockSpec(memory_space=pltpu.VMEM),
            pl.BlockSpec(memory_space=pl.ANY),
            pl.BlockSpec(memory_space=pltpu.VMEM),
        ),
        scratch_shapes=[
            pltpu.VMEM((2, 768, HALF), BF16),
            pltpu.VMEM((384, 768), BF16),
            pltpu.VMEM((768, 384), BF16),
            pltpu.VMEM((2, 384, HALF), F32),
            pltpu.VMEM((2, 2, ROWS, HALF), F32),
            pltpu.VMEM((2, 2, ROWS, HALF), F32),
            pltpu.VMEM((2, 2, 2, ROWS, HALF), F32),
            pltpu.VMEM((2, ROWS, HALF), F32),
            pltpu.VMEM((2, 2, ROWS, HALF), F32),
            pltpu.VMEM((2, 384, HALF), BF16),
            pltpu.VMEM((2, ROWS, HALF), BF16),
            pltpu.VMEM((CHUNKS, 64, 768), BF16),
            pltpu.VMEM((CHUNKS, NX, 16, 768), BF16),
            pltpu.VMEM((CHUNKS, 2, 16, 384), BF16),
            pltpu.VMEM((NZ, 16, 384), BF16),
            pltpu.VMEM((2, 768, HALF), BF16),
            pltpu.VMEM((NX, 8, 128), F32),
            pltpu.VMEM((NZ, 8, 128), F32),
            pltpu.VMEM((CHUNKS, 8, 128), F32),
            dma((3,)), dma((2,)),
            dma((14,)), dma((14,)),
            dma((NX,)), dma((NX,)),
            dma((NZ,)), dma((NZ,)),
            dma((CHUNKS,)), dma((CHUNKS,)),
            dma((14,)), dma((14,)),
            dma((CHUNKS, NX)), dma((CHUNKS, NX)),
            dma((NZ,)), dma((NZ,)),
        ],
        compiler_params=pltpu.CompilerParams(
            collective_id=0, has_side_effects=True, vmem_limit_bytes=48 * 1024 * 1024
        ),
        cost_estimate=pl.CostEstimate(flops=2400000000, bytes_accessed=5000000, transcendentals=400000),
    )(hidden, head_weight, token_ids.reshape(1, 384))


def solution(mesh):
    return jax.shard_map(
        body,
        mesh=mesh,
        in_specs=(P("rep", None, "tok"), P("rep", "tok", "vocab"), P()),
        out_specs=(P("rep", "tok"), P("rep", "tok", "vocab"), P("rep", "vocab", "tok")),
        check_vma=False,
    )
```

```python
import functools

import jax
import jax.numpy as jnp
from jax import lax
from jax.experimental import pallas as pl
from jax.experimental.pallas import tpu as pltpu
from jax.sharding import PartitionSpec as P

F32, BF16, I16, I32 = jnp.float32, jnp.bfloat16, jnp.int16, jnp.int32
NX, NZ, NY = 4, 16, 4
CHUNKS = 8
ROWS = 48
HALF = 640
STEPS = 4
MESH = pl.DeviceIdType.MESH


def rows_of(m):
    return pl.ds(pl.multiple_of(m * ROWS, 16), ROWS)


def dot(a, b, ca, cb):
    return lax.dot_general(a, b, (((ca,), (cb,)), ((), ())), preferred_element_type=F32)


def iota(shape, dim):
    return lax.broadcasted_iota(I32, shape, dim)


def by24(v):
    return (v * 2731) >> 16


def by6(v):
    return (v * 10923) >> 16


def kernel(
    hid, wt, ids, loss_out, wg_out, hg_out,
    id_v, w_v, h_v, hp, ht_v, acc, qf, qd, cbuf, fbuf, rx, pr, lg, sg, s1, hgs, xr, zs, zr,
    sc, xst, zst, zls, lb, perm, spread,
    load_sem, a_send, a_recv, sc_send, sc_recv, st_send, st_recv, zst_send, zst_recv, zls_send, zls_recv,
    l_send, l_recv, g_send, g_recv, x_send, x_recv, z_send, z_recv,
):
    c = lax.axis_index("rep")
    v = lax.axis_index("vocab")
    y = lax.axis_index("tok")
    z, x = v // NX, v % NX
    pc = 1 - c
    R, L, O = (y + 1) % NY, (y + 3) % NY, (y + 2) % NY
    mine = y + 4 * c
    cores = (c, pc)

    def xid(d):
        return {"vocab": z * NX + (x + d) % NX}

    def zid(zz):
        return {"vocab": zz * NX + x}

    def yid(core, yy):
        return {"rep": core, "tok": yy}

    loads = [
        pltpu.make_async_copy(hid.at[0], h_v, load_sem.at[0]),
        pltpu.make_async_copy(wt.at[0, :, pl.ds(0, HALF)], w_v.at[0], load_sem.at[1]),
        pltpu.make_async_copy(wt.at[0, :, pl.ds(HALF, HALF)], w_v.at[1], load_sem.at[2]),
        pltpu.make_async_copy(ids, id_v, load_sem.at[3]),
    ]
    for cp in loads:
        cp.start()

    barrier = pltpu.get_barrier_semaphore()
    peers = [yid(cores[s], yy) for s in range(2) for yy in (y, R, L, O)][1:]
    peers += [xid(d) for d in range(1, NX)] + [zid((z + d) % NZ) for d in range(1, NZ)]
    for p in peers:
        pl.semaphore_signal(barrier, inc=1, device_id=p, device_id_type=MESH)

    def remote(src, dst, ss, rs, dev):
        return pltpu.make_async_remote_copy(
            src_ref=src, dst_ref=dst, send_sem=ss, recv_sem=rs, device_id=dev, device_id_type=MESH
        )

    sends = []

    def start(cp):
        cp.start()
        sends.append(cp)

    lane, tok = iota((ROWS, 128), 1), iota((ROWS, 128), 0)

    def to_row(cols):
        return sum(jnp.sum(jnp.where(lane == tok + 64 * i, cols[i], 0.0), axis=0, keepdims=True) for i in range(2))

    def to_col(row, i):
        return jnp.sum(jnp.where(lane == tok + 64 * i, row, 0.0), axis=1, keepdims=True)

    loads[0].wait()
    hf = h_v[...].astype(F32)
    hp[...] = jnp.concatenate(
        [hf[24 * (m + 8 * q):24 * (m + 8 * q) + 24] for m in range(CHUNKS) for q in range(2)], axis=0
    ).astype(BF16)
    for a in range(2):
        loads[1 + a].wait()
        acc[a] = dot(hp[...], w_v[a], 1, 0)
    top = jnp.maximum(
        jnp.max(jnp.abs(acc[0]), axis=1, keepdims=True), jnp.max(jnp.abs(acc[1]), axis=1, keepdims=True)
    )
    step = jnp.maximum(top, 1e-30) * (1.0 / 32767.0)
    sc[6] = jnp.concatenate(
        [to_row([step[ROWS * (b + 4 * h):ROWS * (b + 4 * h) + ROWS] for h in range(2)]) for b in range(NY)]
        + [jnp.zeros((4, 128), F32)], axis=0,
    )

    def step_of(slot, b, h):
        return to_col(sc[slot, pl.ds(b, 1)], h)

    def coded(value, by):
        return jnp.round(value * (1.0 / by)).astype(I32).astype(I16)

    def decoded(code):
        return code.astype(I32).astype(F32)

    pl.semaphore_wait(barrier, len(peers))
    for j, yy in enumerate((R, L, O)):
        for s in range(2):
            start(remote(sc.at[6], sc.at[3 * s + j], sc_send.at[3 * s + j], sc_recv.at[3 * s + j], yid(cores[s], yy)))
    for kind in range(2):
        for s in range(2):
            for a in range(2):
                near, far = ((R, L), (L, R))[a]
                i = 4 * kind + 2 * a + s
                b = (O, far)[kind]
                code = coded(acc[a, rows_of(b + 4 * cores[s])], step_of(6, b, cores[s]))
                if kind == 0:
                    qf[a, s] = code
                    start(remote(qf.at[a, s], fbuf.at[a, s], a_send.at[i], a_recv.at[i], yid(c, near)))
                else:
                    qd[a, s] = code
                    start(remote(qd.at[a, s], rx.at[0, a, s], a_send.at[i], a_recv.at[i], yid(cores[s], far)))
    for a in range(2):
        start(remote(acc.at[a, rows_of(y + 4 * pc)], pr.at[a], a_send.at[12 + a], a_recv.at[12 + a], yid(pc, y)))

    def got_step(slot):
        remote(sc.at[6], sc.at[slot], sc_send.at[slot], sc_recv.at[slot], yid(pc, y)).wait_recv()

    got_step(0)
    got_step(1)
    for s in range(2):
        for a in range(2):
            i = 2 * a + s
            near = (R, L)[a]
            remote(qf.at[a, s], fbuf.at[a, s], a_send.at[i], a_recv.at[i], yid(c, near)).wait_recv()
            by = step_of(a, near, cores[s])
            value = acc[a, rows_of(near + 4 * cores[s])] + decoded(fbuf[a, s]) * by
            cbuf[a, s] = coded(value, by + step_of(6, near, cores[s]))
            start(remote(cbuf.at[a, s], rx.at[1, a, s], a_send.at[8 + i], a_recv.at[8 + i], yid(cores[s], near)))

    ht_v[...] = hp[...].T
    loads[3].wait()
    t0 = iota((ROWS, 384), 0)
    token = mine * 24 + t0 + jnp.where(t0 >= 24, 168, 0)
    id_col = jnp.sum(jnp.where(iota((ROWS, 384), 1) == token, id_v[...][None, :], 0), axis=1, keepdims=True)
    id_col = id_col - v * (2 * HALF)
    r, t = iota((96, 96), 0), iota((96, 96), 1)
    w = r - by24(r) * 24
    perm[...] = jnp.where(t == by6(w) * 24 + by24(r) * 6 + w - by6(w) * 6, 1.0, 0.0).astype(BF16)
    r, t = iota((64, ROWS), 0), iota((64, ROWS), 1)
    inner = r & 7
    spread[...] = jnp.where((t == ((r >> 3) & 1) * 24 + (r >> 4) * 6 + inner) & (inner < 6), 1.0, 0.0).astype(BF16)

    for a in range(2):
        remote(acc.at[a, rows_of(mine)], pr.at[a], a_send.at[12 + a], a_recv.at[12 + a], yid(pc, y)).wait_recv()
    for slot in range(2, 6):
        got_step(slot)
    for s in range(2):
        steps = [step_of(3 * s + j, y, c) for j in range(3)]
        for a in range(2):
            for k in range(2):
                i = 4 + 4 * k + 2 * a + s
                remote(cbuf.at[a, s], rx.at[k, a, s], a_send.at[i], a_recv.at[i], yid(c, R)).wait_recv()
            own = acc[a, rows_of(mine)] if s == 0 else pr[a]
            lg[s, a] = own + decoded(rx[0, a, s]) * steps[1 - a] + decoded(rx[1, a, s]) * (steps[a] + steps[2])

    cols = iota((ROWS, HALF), 1)
    stats = []
    for s in range(2):
        la, lbh = lg[s, 0], lg[s, 1]
        peak = jnp.maximum(jnp.max(la, axis=1, keepdims=True), jnp.max(lbh, axis=1, keepdims=True))
        tot = [0.0] * 4
        for a, l in ((0, la), (1, lbh)):
            e = jnp.exp((l - peak) * 0.5)
            hit = cols == id_col - a * HALF
            for n, term in enumerate((e * e, e, jnp.where(hit, l, 0.0), e * (0.5 * (l - lg[1 - s, a])))):
                tot[n] = tot[n] + jnp.sum(term, axis=1, keepdims=True)
        stats.append([peak] + tot)
    xst[0] = jnp.concatenate([to_row([stats[s][n] for s in range(2)]) for n in range(5)] + [jnp.zeros((3, 128), F32)], axis=0)
    for d in range(1, NX):
        start(remote(xst.at[0], xst.at[d], st_send.at[d], st_recv.at[d], xid(d)))
    for d in range(1, NX):
        remote(xst.at[0], xst.at[d], st_send.at[d], st_recv.at[d], xid(d)).wait_recv()

    def merge(parts):
        tops = functools.reduce(jnp.maximum, [p[0:1] for p in parts])
        fs = [jnp.exp((p[0:1] - tops) * 0.5) for p in parts]
        return tops, fs, [sum(p[n:n + 1] * f for p, f in zip(parts, ws)) for n, ws in ((1, [f * f for f in fs]), (2, fs))]

    parts = [xst[d] for d in range(NX)]
    tops, fs, (norm, tau) = merge(parts)
    zst[0] = jnp.concatenate([tops, norm, tau, jnp.zeros((1, 128), F32)], axis=0)
    for d in range(1, NZ):
        start(remote(zst.at[0], zst.at[d], zst_send.at[d], zst_recv.at[d], zid((z + d) % NZ)))
    picked = sum(p[3:4] for p in parts)
    apart = sum(p[4:5] * f for p, f in zip(parts, fs))
    zls[0] = jnp.concatenate([picked, apart, jnp.zeros((2, 128), F32)], axis=0)
    for d in range(1, NZ):
        remote(zst.at[0], zst.at[d], zst_send.at[d], zst_recv.at[d], zid((z + d) % NZ)).wait_recv()
    tops, fs, (norm, tau) = merge([zst[d] for d in range(NZ)])
    log_total = tops + jnp.log(norm)
    tau_total = tops * 0.5 + jnp.log(tau)

    mr = rows_of(mine)
    log_col = [to_col(log_total, s) for s in range(2)]
    tau_col = [to_col(tau_total, s) for s in range(2)]

    def grad_copy(s, a, side):
        i = 4 * side + 2 * a + s
        src = sg.at[a, mr] if s == 0 else s1.at[a]
        return remote(src, sg.at[a, mr], g_send.at[i], g_recv.at[i], yid(cores[s], ((R, L), (L, R))[side][a]))

    for a in range(2):
        hit = jnp.where(cols == id_col - a * HALF, 1.0, 0.0)
        l = [lg[0, a], lg[1, a]]
        q = [jnp.exp(l[s] * 0.5 - tau_col[s]) for s in range(2)]
        for s in range(2):
            g = (jnp.exp(l[s] - log_col[s]) - hit + (q[s] - q[1 - s])).astype(BF16)
            if s == 0:
                sg[a, mr] = g
            else:
                s1[a] = g
        start(grad_copy(0, a, 0))
    for a in range(2):
        start(remote(s1.at[a], sg.at[a, mr], g_send.at[12 + a], g_recv.at[12 + a], yid(pc, y)))
        start(grad_copy(0, a, 1))
    for side in range(2):
        for a in range(2):
            start(grad_copy(1, a, side))
    for d in range(1, NZ):
        start(remote(zls.at[0], zls.at[d], zls_send.at[d], zls_recv.at[d], zid((z + d) % NZ)))

    pairs = [(mine, y + 4 * pc)] + [(L + 4 * cores[s], R + 4 * cores[s]) for s in range(2)] + [(O + 4 * c, O + 4 * pc)]

    def hidden_part(k):
        part = sum(
            dot(jnp.concatenate([sg[a, rows_of(m)] for m in pairs[k]], axis=0), w_v[a], 1, 1) for a in range(2)
        )
        part = dot(perm[...], part.astype(BF16), 1, 0)
        for n in range(NX):
            p = part[24 * n:24 * n + 24]
            hgs[k, n] = jnp.concatenate([p[:, :384], p[:, 384:]], axis=0).astype(BF16)
        for d in (2, 1, 3):
            start(remote(hgs.at[k, (x + d) % NX], xr.at[k, d], x_send.at[k, d], x_recv.at[k, d], xid(d)))

    def x_sum(k):
        total = hgs[k, x].astype(F32)
        for d in range(1, NX):
            remote(hgs.at[k, 0], xr.at[k, d], x_send.at[k, d], x_recv.at[k, d], xid(d)).wait_recv()
            total = total + xr[k, d].astype(F32)
        zs[k] = dot(spread[...], total.astype(BF16), 1, 0).astype(BF16)
        for g in range(4):
            zz = pairs[k][g // 2] + 8 * (g % 2)
            d = (zz - z + NZ) % NZ

            @pl.when(d != 0)
            def _():
                remote(zs.at[k, pl.ds(16 * g, 16)], zr.at[d], z_send.at[d], z_recv.at[d], zid(zz)).start()

            @pl.when(d == 0)
            def _():
                zr[0] = zs[k, 16 * g:16 * g + 16]

    def got(i, a, m):
        remote(sg.at[a, rows_of(m)], sg.at[a, rows_of(m)], g_send.at[i], g_recv.at[i], yid(c, L)).wait_recv()

    def forward(s):
        for a in range(2):
            m = (L, R)[a] + 4 * cores[s]
            got(2 * a + s, a, m)
            i = 8 + 2 * a + s
            start(remote(sg.at[a, rows_of(m)], sg.at[a, rows_of(m)], g_send.at[i], g_recv.at[i], yid(c, (R, L)[a])))

    def rest(s):
        for a in range(2):
            got(4 + 2 * a + s, a, (R, L)[a] + 4 * cores[s])

    for a in range(2):
        got(12 + a, a, pairs[0][1])
    hidden_part(0)
    forward(0)
    rest(0)
    hidden_part(1)
    forward(1)
    x_sum(0)
    rest(1)
    hidden_part(2)
    x_sum(1)

    for d in range(1, NZ):
        remote(zls.at[0], zls.at[d], zls_send.at[d], zls_recv.at[d], zid((z + d) % NZ)).wait_recv()
    late = [zls[d] for d in range(NZ)]
    picked = sum(p[0:1] for p in late)
    apart = sum(p[1:2] * f for p, f in zip(late, fs))
    ratio = pltpu.roll(apart / tau - tau_total, 64, 1) + tau_total
    loss = log_total - picked + 2.0 * ratio
    lb[mine] = jnp.concatenate([loss, jnp.zeros((7, 128), F32)], axis=0)
    for e in range(1, CHUNKS):
        m = (mine + e) % CHUNKS
        start(remote(lb.at[mine], lb.at[mine], l_send.at[e], l_recv.at[mine], yid(m // 4, m % 4)))

    for s in range(2):
        for a in range(2):
            got(8 + 2 * a + s, a, O + 4 * cores[s])
    hidden_part(3)
    x_sum(2)
    for a in range(2):
        wg_out[0, :, a * HALF:(a + 1) * HALF] = dot(ht_v[...], sg[a], 1, 0).astype(BF16)
        if a == 0:
            x_sum(3)

    for e in range(1, CHUNKS):
        m = (mine + e) % CHUNKS
        remote(lb.at[m], lb.at[m], l_send.at[e], l_recv.at[m], yid(pc, y)).wait_recv()
    lanes = iota((1, 128), 1)
    mixed = jnp.zeros((1, 128), F32)
    for i in range(4):
        m = (4 * y + i) % CHUNKS
        row = lb[m, 0:1]
        row = jnp.where(m // 4 == c, row, pltpu.roll(row, 64, 1))
        row = jnp.where(y // 2 == 0, row, pltpu.roll(row, 104, 1))
        if i:
            row = pltpu.roll(row, 24 * i, 1)
        mixed = jnp.where((lanes >= 24 * i) & (lanes < 24 * i + 24), row, mixed)
    loss_out[...] = mixed[:, :96]

    for d in range(1, NZ):
        remote(zr.at[d], zr.at[d], z_send.at[d], z_recv.at[d], zid(z)).wait_recv()
    total = sum(zr[d].astype(F32) for d in range(NZ))
    hg_out[0] = jnp.concatenate([total[:8], total[8:]], axis=1)[:6].astype(BF16)

    for cp in sends:
        cp.wait_send()
    for d in range(1, NZ):
        remote(zr.at[d], zr.at[d], z_send.at[d], z_recv.at[d], zid((z + d) % NZ)).wait_send()


def finish(*refs):
    copies = [pltpu.make_async_copy(refs[i], refs[3 + i], refs[6].at[i]) for i in range(3)]
    for cp in copies:
        cp.start()
    for cp in copies:
        cp.wait()


def body(hidden, head_weight, token_ids):
    dma = pltpu.SemaphoreType.DMA
    outs = pl.pallas_call(
        kernel,
        out_shape=(
            pltpu.VMEM((1, 96), F32),
            pltpu.VMEM((1, 768, 2 * HALF), BF16),
            pltpu.VMEM((1, 6, 768), BF16),
        ),
        in_specs=[pl.BlockSpec(memory_space=pl.ANY)] * 3,
        out_specs=(pl.BlockSpec(memory_space=pltpu.VMEM),) * 3,
        scratch_shapes=[
            pltpu.VMEM((384,), I32),
            pltpu.VMEM((2, 768, HALF), BF16),
            pltpu.VMEM((384, 768), BF16),
            pltpu.VMEM((384, 768), BF16),
            pltpu.VMEM((768, 384), BF16),
            pltpu.VMEM((2, 384, HALF), F32),
            pltpu.VMEM((2, 2, ROWS, HALF), I16),
            pltpu.VMEM((2, 2, ROWS, HALF), I16),
            pltpu.VMEM((2, 2, ROWS, HALF), I16),
            pltpu.VMEM((2, 2, ROWS, HALF), I16),
            pltpu.VMEM((2, 2, 2, ROWS, HALF), I16),
            pltpu.VMEM((2, ROWS, HALF), F32),
            pltpu.VMEM((2, 2, ROWS, HALF), F32),
            pltpu.VMEM((2, 384, HALF), BF16),
            pltpu.VMEM((2, ROWS, HALF), BF16),
            pltpu.VMEM((STEPS, NX, ROWS, 384), BF16),
            pltpu.VMEM((STEPS, NX, ROWS, 384), BF16),
            pltpu.VMEM((STEPS, 64, 384), BF16),
            pltpu.VMEM((NZ, 16, 384), BF16),
            pltpu.VMEM((7, 8, 128), F32),
            pltpu.VMEM((NX, 8, 128), F32),
            pltpu.VMEM((NZ, 4, 128), F32),
            pltpu.VMEM((NZ, 4, 128), F32),
            pltpu.VMEM((CHUNKS, 8, 128), F32),
            pltpu.VMEM((96, 96), BF16),
            pltpu.VMEM((64, ROWS), BF16),
            dma((4,)),
            dma((14,)), dma((14,)),
            dma((6,)), dma((6,)),
            dma((NX,)), dma((NX,)),
            dma((NZ,)), dma((NZ,)),
            dma((NZ,)), dma((NZ,)),
            dma((CHUNKS,)), dma((CHUNKS,)),
            dma((14,)), dma((14,)),
            dma((STEPS, NX)), dma((STEPS, NX)),
            dma((NZ,)), dma((NZ,)),
        ],
        compiler_params=pltpu.CompilerParams(
            collective_id=0, has_side_effects=True, vmem_limit_bytes=60 * 1024 * 1024
        ),
        cost_estimate=pl.CostEstimate(flops=2400000000, bytes_accessed=5000000, transcendentals=400000),
    )(hidden, head_weight, token_ids)
    return pl.pallas_call(
        finish,
        out_shape=tuple(jax.ShapeDtypeStruct(o.shape, o.dtype) for o in outs),
        in_specs=[pl.BlockSpec(memory_space=pltpu.VMEM)] * 3,
        out_specs=(pl.BlockSpec(memory_space=pl.ANY),) * 3,
        scratch_shapes=[dma((3,))],
        compiler_params=pltpu.CompilerParams(vmem_limit_bytes=1024 * 1024),
    )(*outs)


def solution(mesh):
    return jax.shard_map(
        body,
        mesh=mesh,
        in_specs=(P("rep", None, "tok"), P("rep", "tok", "vocab"), P()),
        out_specs=(P("rep", "tok"), P("rep", "tok", "vocab"), P("rep", "vocab", "tok")),
        check_vma=False,
    )
```

```python
import functools

import jax
import jax.numpy as jnp
from jax import lax
from jax.experimental import pallas as pl
from jax.experimental.pallas import tpu as pltpu
from jax.sharding import PartitionSpec as P

F32, BF16, I16, I32 = jnp.float32, jnp.bfloat16, jnp.int16, jnp.int32
NX, NZ, NY = 4, 16, 4
CHUNKS = 8
ROWS = 48
HALF = 640
PAIRS = 3
MESH = pl.DeviceIdType.MESH


def rows_of(m):
    return pl.ds(pl.multiple_of(m * ROWS, 16), ROWS)


def dot(a, b, ca, cb):
    return lax.dot_general(a, b, (((ca,), (cb,)), ((), ())), preferred_element_type=F32)


def iota(shape, dim):
    return lax.broadcasted_iota(I32, shape, dim)


def by24(v):
    return (v * 2731) >> 16


def by6(v):
    return (v * 10923) >> 16


def kernel(
    hid, wt, ids, loss_out, wg_out, hg_out,
    id_v, w_v, wt_v, h_v, hp, ht_v, acc, qf, qd, cbuf, fbuf, rx, pr, lg, sg, s1, hgs, xr, zs, zr,
    hgt, xrt, zst2, sc, xst, zst, zls, lb, perm, spread, perm1, spread1, ev,
    load_sem, a_send, a_recv, sc_send, sc_recv, st_sem, zst_sem, zls_sem, l_sem, g_send, g_recv, x_send, x_recv, z_sem,
):
    c = lax.axis_index("rep")
    v = lax.axis_index("vocab")
    y = lax.axis_index("tok")
    z, x = v // NX, v % NX
    pc = 1 - c
    R, L, O = (y + 1) % NY, (y + 3) % NY, (y + 2) % NY
    mine = y + 4 * c
    cores = (c, pc)

    def xid(d):
        return {"vocab": z * NX + (x + d) % NX}

    def zid(zz):
        return {"vocab": zz * NX + x}

    def yid(core, yy):
        return {"rep": core, "tok": yy}

    loads = [
        pltpu.make_async_copy(hid.at[0], h_v, load_sem.at[0]),
        pltpu.make_async_copy(wt.at[0, :, pl.ds(0, HALF)], w_v.at[0], load_sem.at[1]),
        pltpu.make_async_copy(wt.at[0, :, pl.ds(HALF, HALF)], w_v.at[1], load_sem.at[2]),
        pltpu.make_async_copy(ids, id_v, load_sem.at[3]),
    ]
    for cp in loads:
        cp.start()

    barrier = pltpu.get_barrier_semaphore()
    peers = [yid(cores[s], yy) for s in range(2) for yy in (y, R, L, O)][1:]
    peers += [xid(d) for d in range(1, NX)] + [zid((z + d) % NZ) for d in range(1, NZ)]
    for p in peers:
        pl.semaphore_signal(barrier, inc=1, device_id=p, device_id_type=MESH)

    def remote(src, dst, ss, rs, dev):
        return pltpu.make_async_remote_copy(
            src_ref=src, dst_ref=dst, send_sem=ss, recv_sem=rs, device_id=dev, device_id_type=MESH
        )

    def start(*copy):
        remote(*copy).start()

    def wait_in(ref, sem):
        remote(ref, ref, sem, sem, yid(pc, y)).wait_recv()

    def wait_out(ref, sem):
        remote(ref, ref, sem, sem, yid(pc, y)).wait_send()

    lane, tok = iota((ROWS, 128), 1), iota((ROWS, 128), 0)

    def to_row(cols, where=(0, 1)):
        return sum(
            jnp.sum(jnp.where(lane == tok + 64 * where[i], cols[i], 0.0), axis=0, keepdims=True) for i in range(2)
        )

    def to_col(row, i):
        return jnp.sum(jnp.where(lane == tok + 64 * i, row, 0.0), axis=1, keepdims=True)

    loads[0].wait()
    hf = h_v[...].astype(F32)
    hp[...] = jnp.concatenate(
        [hf[24 * (m + 8 * q):24 * (m + 8 * q) + 24] for m in range(CHUNKS) for q in range(2)], axis=0
    ).astype(BF16)
    for a in range(2):
        loads[1 + a].wait()

    def step_of(slot, b, h):
        return to_col(sc[slot, pl.ds(b, 1)], h)

    def coded(value, by):
        return jnp.round(value * (1.0 / by)).astype(I32).astype(I16)

    def decoded(code):
        return code.astype(I32).astype(F32)

    sc[6] = jnp.zeros((8, 128), F32)
    own = {}
    place = {"R": R, "L": L, "O": O, "y": y}

    def logits(owners):
        chunks = [(name, s) for name in owners for s in range(2)]
        ms = [rows_of(place[name] + 4 * cores[s]) for name, s in chunks]
        lhs = jnp.concatenate([hp[m] for m in ms], axis=0)
        parts = [dot(lhs, w_v[a], 1, 0) for a in range(2)]
        top = jnp.maximum(*[jnp.max(jnp.abs(p), axis=1, keepdims=True) for p in parts])
        step = jnp.maximum(top, 1e-30) * (1.0 / 32767.0)
        for n, m in enumerate(ms):
            here = slice(ROWS * n, ROWS * n + ROWS)
            for a in range(2):
                acc[a, m] = parts[a][here]
            own[chunks[n]] = step[here]
        for name in owners:
            sc[6, pl.ds(place[name], 1)] = to_row([own[name, s] for s in range(2)], cores)

    def send_coded(kind):
        for s in range(2):
            for a in range(2):
                near, far = ((R, L), (L, R))[a]
                name = ("O", "LR"[a])[kind]
                code = coded(acc[a, rows_of(place[name] + 4 * cores[s])], own[name, s])
                if kind == 0:
                    qf[a, s] = code
                    start(qf.at[a, s], fbuf.at[s, a], a_send.at[0], a_recv.at[s], yid(c, near))
                else:
                    qd[a, s] = code
                    start(qd.at[a, s], rx.at[s, 0, a], a_send.at[1], a_recv.at[2 + s], yid(cores[s], far))

    logits("O")
    pl.semaphore_wait(barrier, len(peers))
    send_coded(0)
    logits("RLy")
    for j, yy in enumerate((R, L, O)):
        for s in range(2):
            late = 1 if s or j == 2 else 0
            start(sc.at[6], sc.at[(0, 1, 4, 2, 3, 5)[3 * s + j]], sc_send.at[0], sc_recv.at[late], yid(cores[s], yy))
    slot = lambda s, j: (0, 1, 4, 2, 3, 5)[3 * s + j]
    send_coded(1)
    for a in range(2):
        start(acc.at[a, rows_of(y + 4 * pc)], pr.at[a], a_send.at[3], a_recv.at[4], yid(pc, y))

    for a in range(2):
        wt_v[a] = w_v[a].T

    wait_in(sc.at[pl.ds(0, 2)], sc_recv.at[0])
    for s in range(2):
        wait_in(fbuf.at[s], a_recv.at[s])
        for a in range(2):
            near = (R, L)[a]
            by = step_of(slot(0, a), near, cores[s])
            value = acc[a, rows_of(near + 4 * cores[s])] + decoded(fbuf[s, a]) * by
            cbuf[a, s] = coded(value, by + own["RL"[a], s])
            start(cbuf.at[a, s], rx.at[s, 1, a], a_send.at[2], a_recv.at[2 + s], yid(cores[s], near))

    ht_v[...] = hp[...].T
    loads[3].wait()
    t0 = iota((ROWS, 384), 0)
    token = mine * 24 + t0 + jnp.where(t0 >= 24, 168, 0)
    id_col = jnp.sum(jnp.where(iota((ROWS, 384), 1) == token, id_v[...][None, :], 0), axis=1, keepdims=True)
    id_col = id_col - v * (2 * HALF)
    r, t = iota((96, 96), 0), iota((96, 96), 1)
    w = r - by24(r) * 24
    perm[...] = jnp.where(t == by6(w) * 24 + by24(r) * 6 + w - by6(w) * 6, 1.0, 0.0).astype(BF16)
    r, t = iota((64, ROWS), 0), iota((64, ROWS), 1)
    inner = r & 7
    spread[...] = jnp.where((t == ((r >> 3) & 1) * 24 + (r >> 4) * 6 + inner) & (inner < 6), 1.0, 0.0).astype(BF16)

    r, t = iota((64, ROWS), 0), iota((64, ROWS), 1)
    w = r & 15
    perm1[...] = jnp.where((t == by6(w) * 24 + (r >> 4) * 6 + w - by6(w) * 6) & (w < 12), 1.0, 0.0).astype(BF16)
    r, t = iota((32, 32), 0), iota((32, 32), 1)
    inner = r & 7
    spread1[...] = jnp.where((t == ((r >> 3) & 1) * 16 + (r >> 4) * 6 + inner) & (inner < 6), 1.0, 0.0).astype(BF16)

    wait_in(pr, a_recv.at[4])
    wait_in(sc.at[pl.ds(2, 4)], sc_recv.at[1])
    cols = iota((ROWS, HALF), 1)
    stats = []
    for s in range(2):
        steps = [step_of(slot(s, j), y, c) for j in range(3)]
        wait_in(rx.at[s], a_recv.at[2 + s])
        for a in range(2):
            base = acc[a, rows_of(mine)] if s == 0 else pr[a]
            lg[s, a] = base + decoded(rx[s, 0, a]) * steps[1 - a] + decoded(rx[s, 1, a]) * (steps[a] + steps[2])
        peak = jnp.maximum(*[jnp.max(lg[s, a], axis=1, keepdims=True) for a in range(2)])
        tot = [0.0] * 3
        for a in range(2):
            l = lg[s, a]
            e = jnp.exp((l - peak) * 0.5)
            ev[s, a] = e
            hit = cols == id_col - a * HALF
            for n, term in enumerate((e * e, e, jnp.where(hit, l, 0.0))):
                tot[n] = tot[n] + jnp.sum(term, axis=1, keepdims=True)
        stats.append([peak] + tot)
    for s in range(2):
        stats[s].append(sum(
            jnp.sum(ev[s, a] * (0.5 * (lg[s, a] - lg[1 - s, a])), axis=1, keepdims=True) for a in range(2)
        ))
    xst[0] = jnp.concatenate([to_row([stats[s][n] for s in range(2)]) for n in range(5)] + [jnp.zeros((3, 128), F32)], axis=0)
    for d in range(1, NX):
        start(xst.at[0], xst.at[d], st_sem.at[0], st_sem.at[1], xid(d))
    wait_in(xst.at[pl.ds(1, NX - 1)], st_sem.at[1])

    def merge(parts):
        tops = functools.reduce(jnp.maximum, [p[0:1] for p in parts])
        fs = [jnp.exp((p[0:1] - tops) * 0.5) for p in parts]
        return tops, fs, [sum(p[n:n + 1] * f for p, f in zip(parts, ws)) for n, ws in ((1, [f * f for f in fs]), (2, fs))]

    parts = [xst[d] for d in range(NX)]
    tops, fs, (norm, tau) = merge(parts)
    zst[0] = jnp.concatenate([tops, norm, tau, jnp.zeros((1, 128), F32)], axis=0)
    for d in range(1, NZ):
        start(zst.at[0], zst.at[d], zst_sem.at[0], zst_sem.at[1], zid((z + d) % NZ))
    picked = sum(p[3:4] for p in parts)
    apart = sum(p[4:5] * f for p, f in zip(parts, fs))
    zls[0] = jnp.concatenate([picked, apart, jnp.zeros((2, 128), F32)], axis=0)
    wait_in(zst.at[pl.ds(1, NZ - 1)], zst_sem.at[1])
    tops, fs, (norm, tau) = merge([zst[d] for d in range(NZ)])
    log_total = tops + jnp.log(norm)
    tau_total = tops * 0.5 + jnp.log(tau)

    mr = rows_of(mine)
    log_col = [to_col(log_total, s) for s in range(2)]
    tau_col = [to_col(tau_total, s) for s in range(2)]

    def send_grad(s, a, side):
        src = sg.at[a, mr] if s == 0 else s1.at[a]
        start(src, sg.at[a, mr], g_send.at[1 - s], g_recv.at[2 * side + s], yid(cores[s], ((R, L), (L, R))[side][a]))

    for a in range(2):
        hit = jnp.where(cols == id_col - a * HALF, 1.0, 0.0)
        l = [lg[0, a], lg[1, a]]
        q = [jnp.exp(l[s] * 0.5 - tau_col[s]) for s in range(2)]
        for s in range(2):
            g = (jnp.exp(l[s] - log_col[s]) - hit + (q[s] - q[1 - s])).astype(BF16)
            if s == 0:
                sg[a, mr] = g
            else:
                s1[a] = g
        send_grad(0, a, 0)
    for a in range(2):
        start(s1.at[a], sg.at[a, mr], g_send.at[0], g_recv.at[4], yid(pc, y))
        send_grad(0, a, 1)
    for d in range(1, NZ):
        start(zls.at[0], zls.at[d], zls_sem.at[0], zls_sem.at[1], zid((z + d) % NZ))

    steps = [(mine, y + 4 * pc)] + [(L + 4 * cores[s], R + 4 * cores[s]) for s in range(2)]
    steps += [(O + 4 * cores[s],) for s in range(2)]

    def buffers(k):
        return (hgs, xr, zs, perm, spread, k, ROWS) if k < PAIRS else (hgt, xrt, zst2, perm1, spread1, k - PAIRS, 32)

    def hidden_part(k):
        hg, xb, _, order, _, n, rows = buffers(k)
        part = sum(
            dot(jnp.concatenate([sg[a, rows_of(m)] for m in steps[k]], axis=0), wt_v[a], 1, 0) for a in range(2)
        )
        part = dot(order[...], part.astype(BF16), 1, 0)
        for q in range(NX):
            p = part[rows // 2 * q:rows // 2 * q + rows // 2]
            hg[n, q] = jnp.concatenate([p[:, :384], p[:, 384:]], axis=0).astype(BF16)
        for d in (2, 1, 3):
            start(hg.at[n, (x + d) % NX], xb.at[n, d], x_send.at[k // PAIRS], x_recv.at[k], xid(d))

    def x_sum(k):
        hg, xb, zb, _, order, n, rows = buffers(k)
        wait_in(xb.at[n, pl.ds(1, NX - 1)], x_recv.at[k])
        total = hg[n, x].astype(F32)
        for d in range(1, NX):
            total = total + xb[n, d].astype(F32)
        zb[n] = dot(order[...], total.astype(BF16), 1, 0).astype(BF16)
        for g in range(2 * len(steps[k])):
            zz = steps[k][g // 2] + 8 * (g % 2)
            d = (zz - z + NZ) % NZ

            @pl.when(d != 0)
            def _():
                start(zb.at[n, pl.ds(16 * g, 16)], zr.at[d], z_sem.at[0], z_sem.at[1], zid(zz))

            @pl.when(d == 0)
            def _():
                zr[0] = zb[n, 16 * g:16 * g + 16]

    def two(m):
        return sg.at[:, rows_of(m)]

    def forward(s):
        wait_in(two(L + 4 * cores[s]), g_recv.at[s])
        for a in range(2):
            m = rows_of((L, R)[a] + 4 * cores[s])
            start(sg.at[a, m], sg.at[a, m], g_send.at[0], g_recv.at[5 + s], yid(c, (R, L)[a]))

    wait_in(two(y + 4 * pc), g_recv.at[4])
    hidden_part(0)
    wait_out(sg.at[:, pl.ds(0, 2 * ROWS)], g_send.at[1])
    for side in range(2):
        for a in range(2):
            send_grad(1, a, side)
    for s in range(2):
        forward(s)
        wait_in(two(L + 4 * cores[s]), g_recv.at[2 + s])
        hidden_part(1 + s)
        x_sum(s)

    wait_in(zls.at[pl.ds(1, NZ - 1)], zls_sem.at[1])
    late = [zls[d] for d in range(NZ)]
    picked = sum(p[0:1] for p in late)
    apart = sum(p[1:2] * f for p, f in zip(late, fs))
    ratio = pltpu.roll(apart / tau - tau_total, 64, 1) + tau_total
    loss = log_total - picked + 2.0 * ratio
    lb[0] = jnp.concatenate([loss, jnp.zeros((7, 128), F32)], axis=0)
    for e in range(1, CHUNKS):
        m = (mine + e) % CHUNKS
        start(lb.at[0], lb.at[e], l_sem.at[0], l_sem.at[1], yid(m // 4, m % 4))
    for s in range(2):
        wait_in(two(O + 4 * cores[s]), g_recv.at[5 + s])
        hidden_part(3 + s)
    x_sum(2)
    for a in range(2):
        wg_out[0, :, a * HALF:(a + 1) * HALF] = dot(ht_v[...], sg[a], 1, 0).astype(BF16)
        x_sum(3 + a)

    wait_in(lb.at[pl.ds(1, CHUNKS - 1)], l_sem.at[1])
    lanes = iota((1, 128), 1)
    mixed = jnp.zeros((1, 128), F32)
    for i in range(4):
        m = (4 * y + i) % CHUNKS
        row = lb[(mine - m + CHUNKS) % CHUNKS, 0:1]
        row = jnp.where(m // 4 == c, row, pltpu.roll(row, 64, 1))
        row = jnp.where(y // 2 == 0, row, pltpu.roll(row, 104, 1))
        if i:
            row = pltpu.roll(row, 24 * i, 1)
        mixed = jnp.where((lanes >= 24 * i) & (lanes < 24 * i + 24), row, mixed)
    loss_out[...] = mixed[:, :96]

    wait_in(zr.at[pl.ds(1, NZ - 1)], z_sem.at[1])
    total = sum(zr[d].astype(F32) for d in range(NZ))
    hg_out[0] = jnp.concatenate([total[:8], total[8:]], axis=1)[:6].astype(BF16)

    wait_out(qf, a_send.at[0])
    wait_out(qd, a_send.at[1])
    wait_out(cbuf, a_send.at[2])
    wait_out(pr, a_send.at[3])
    wait_out(sc.at[pl.ds(0, 6)], sc_send.at[0])
    wait_out(xst.at[pl.ds(1, NX - 1)], st_sem.at[0])
    wait_out(zst.at[pl.ds(1, NZ - 1)], zst_sem.at[0])
    wait_out(zls.at[pl.ds(1, NZ - 1)], zls_sem.at[0])
    wait_out(lb.at[pl.ds(1, CHUNKS - 1)], l_sem.at[0])
    wait_out(sg.at[:, pl.ds(0, 5 * ROWS)], g_send.at[0])
    wait_out(xr.at[:, pl.ds(1, NX - 1)], x_send.at[0])
    wait_out(xrt.at[:, pl.ds(1, NX - 1)], x_send.at[1])
    wait_out(zr.at[pl.ds(1, NZ - 1)], z_sem.at[0])


def finish(*refs):
    copies = [pltpu.make_async_copy(refs[i], refs[3 + i], refs[6].at[i]) for i in range(3)]
    for cp in copies:
        cp.start()
    for cp in copies:
        cp.wait()


def body(hidden, head_weight, token_ids):
    dma = pltpu.SemaphoreType.DMA
    outs = pl.pallas_call(
        kernel,
        out_shape=(
            pltpu.VMEM((1, 96), F32),
            pltpu.VMEM((1, 768, 2 * HALF), BF16),
            pltpu.VMEM((1, 6, 768), BF16),
        ),
        in_specs=[pl.BlockSpec(memory_space=pl.ANY)] * 3,
        out_specs=(pl.BlockSpec(memory_space=pltpu.VMEM),) * 3,
        scratch_shapes=[
            pltpu.VMEM((384,), I32),
            pltpu.VMEM((2, 768, HALF), BF16),
            pltpu.VMEM((2, HALF, 768), BF16),
            pltpu.VMEM((384, 768), BF16),
            pltpu.VMEM((384, 768), BF16),
            pltpu.VMEM((768, 384), BF16),
            pltpu.VMEM((2, 384, HALF), F32),
            pltpu.VMEM((2, 2, ROWS, HALF), I16),
            pltpu.VMEM((2, 2, ROWS, HALF), I16),
            pltpu.VMEM((2, 2, ROWS, HALF), I16),
            pltpu.VMEM((2, 2, ROWS, HALF), I16),
            pltpu.VMEM((2, 2, 2, ROWS, HALF), I16),
            pltpu.VMEM((2, ROWS, HALF), F32),
            pltpu.VMEM((2, 2, ROWS, HALF), F32),
            pltpu.VMEM((2, 384, HALF), BF16),
            pltpu.VMEM((2, ROWS, HALF), BF16),
            pltpu.VMEM((PAIRS, NX, ROWS, 384), BF16),
            pltpu.VMEM((PAIRS, NX, ROWS, 384), BF16),
            pltpu.VMEM((PAIRS, 64, 384), BF16),
            pltpu.VMEM((NZ, 16, 384), BF16),
            pltpu.VMEM((2, NX, 32, 384), BF16),
            pltpu.VMEM((2, NX, 32, 384), BF16),
            pltpu.VMEM((2, 32, 384), BF16),
            pltpu.VMEM((7, 8, 128), F32),
            pltpu.VMEM((NX, 8, 128), F32),
            pltpu.VMEM((NZ, 4, 128), F32),
            pltpu.VMEM((NZ, 4, 128), F32),
            pltpu.VMEM((CHUNKS, 8, 128), F32),
            pltpu.VMEM((96, 96), BF16),
            pltpu.VMEM((64, ROWS), BF16),
            pltpu.VMEM((64, ROWS), BF16),
            pltpu.VMEM((32, 32), BF16),
            pltpu.VMEM((2, 2, ROWS, HALF), F32),
            dma((4,)),
            dma((4,)), dma((5,)),
            dma((1,)), dma((2,)),
            dma((2,)), dma((2,)), dma((2,)), dma((2,)),
            dma((2,)), dma((7,)),
            dma((2,)), dma((PAIRS + 2,)),
            dma((2,)),
        ],
        compiler_params=pltpu.CompilerParams(
            collective_id=0, has_side_effects=True, vmem_limit_bytes=60 * 1024 * 1024
        ),
        cost_estimate=pl.CostEstimate(flops=2400000000, bytes_accessed=5000000, transcendentals=400000),
    )(hidden, head_weight, token_ids)
    return pl.pallas_call(
        finish,
        out_shape=tuple(jax.ShapeDtypeStruct(o.shape, o.dtype) for o in outs),
        in_specs=[pl.BlockSpec(memory_space=pltpu.VMEM)] * 3,
        out_specs=(pl.BlockSpec(memory_space=pl.ANY),) * 3,
        scratch_shapes=[dma((3,))],
        compiler_params=pltpu.CompilerParams(vmem_limit_bytes=1024 * 1024),
    )(*outs)


def solution(mesh):
    return jax.shard_map(
        body,
        mesh=mesh,
        in_specs=(P("rep", None, "tok"), P("rep", "tok", "vocab"), P()),
        out_specs=(P("rep", "tok"), P("rep", "tok", "vocab"), P("rep", "vocab", "tok")),
        check_vma=False,
    )
```

```python
import functools

import jax
import jax.numpy as jnp
from jax import lax
from jax.experimental import pallas as pl
from jax.experimental.pallas import tpu as pltpu
from jax.sharding import PartitionSpec as P

F32, BF16, I16, I32 = jnp.float32, jnp.bfloat16, jnp.int16, jnp.int32
NX, NZ, NY = 4, 16, 4
CHUNKS = 8
ROWS = 48
HALF = 640
PAIRS = 3
MESH = pl.DeviceIdType.MESH


def rows_of(m):
    return pl.ds(pl.multiple_of(m * ROWS, 16), ROWS)


def dot(a, b, ca, cb):
    return lax.dot_general(a, b, (((ca,), (cb,)), ((), ())), preferred_element_type=F32)


def iota(shape, dim):
    return lax.broadcasted_iota(I32, shape, dim)


def by24(v):
    return (v * 2731) >> 16


def by6(v):
    return (v * 10923) >> 16


def kernel(
    hid, wt, ids, loss_out, wg_out, hg_out,
    id_v, w_v, wt_v, h_v, hp, ht_v, acc, qf, qd, cbuf, fbuf, rx, pr, lg, sg, s1, hgs, xr, zs, zr,
    hgt, xrt, zst2, sc, sce, xst, zst, zls, lb, perm, spread, perm1, spread1, ev,
    load_sem, a_send, a_recv, sc_send, sc_recv, st_sem, zst_sem, zls_sem, l_sem, g_send, g_recv, x_send, x_recv, z_sem,
):
    c = lax.axis_index("rep")
    v = lax.axis_index("vocab")
    y = lax.axis_index("tok")
    z, x = v // NX, v % NX
    pc = 1 - c
    R, L, O = (y + 1) % NY, (y + 3) % NY, (y + 2) % NY
    mine = y + 4 * c
    cores = (c, pc)

    def xid(d):
        return {"vocab": z * NX + (x + d) % NX}

    def zid(zz):
        return {"vocab": zz * NX + x}

    def yid(core, yy):
        return {"rep": core, "tok": yy}

    loads = [
        pltpu.make_async_copy(hid.at[0], h_v, load_sem.at[0]),
        pltpu.make_async_copy(wt.at[0, :, pl.ds(0, HALF)], w_v.at[0], load_sem.at[1]),
        pltpu.make_async_copy(wt.at[0, :, pl.ds(HALF, HALF)], w_v.at[1], load_sem.at[2]),
        pltpu.make_async_copy(ids, id_v, load_sem.at[3]),
    ]
    for cp in loads:
        cp.start()

    barrier = pltpu.get_barrier_semaphore()
    peers = [yid(cores[s], yy) for s in range(2) for yy in (y, R, L, O)][1:]
    peers += [xid(d) for d in range(1, NX)] + [zid((z + d) % NZ) for d in range(1, NZ)]
    for p in peers:
        pl.semaphore_signal(barrier, inc=1, device_id=p, device_id_type=MESH)

    def remote(src, dst, ss, rs, dev):
        return pltpu.make_async_remote_copy(
            src_ref=src, dst_ref=dst, send_sem=ss, recv_sem=rs, device_id=dev, device_id_type=MESH
        )

    def start(*copy):
        remote(*copy).start()

    def wait_in(ref, sem):
        remote(ref, ref, sem, sem, yid(pc, y)).wait_recv()

    def wait_out(ref, sem):
        remote(ref, ref, sem, sem, yid(pc, y)).wait_send()

    lane, tok = iota((ROWS, 128), 1), iota((ROWS, 128), 0)

    def to_row(cols, where=(0, 1)):
        return sum(
            jnp.sum(jnp.where(lane == tok + 64 * where[i], cols[i], 0.0), axis=0, keepdims=True) for i in range(2)
        )

    def to_col(row, i):
        return jnp.sum(jnp.where(lane == tok + 64 * i, row, 0.0), axis=1, keepdims=True)

    loads[0].wait()
    hf = h_v[...].astype(F32)
    hp[...] = jnp.concatenate(
        [hf[24 * (m + 8 * q):24 * (m + 8 * q) + 24] for m in range(CHUNKS) for q in range(2)], axis=0
    ).astype(BF16)
    for a in range(2):
        loads[1 + a].wait()

    def step_of(slot, b, h):
        return to_col(sc[slot, pl.ds(b, 1)], h)

    def coded(value, by):
        return jnp.round(value * (1.0 / by)).astype(I32).astype(I16)

    def decoded(code):
        return code.astype(I32).astype(F32)

    sc[6] = jnp.zeros((8, 128), F32)
    own = {}
    place = {"R": R, "L": L, "O": O, "y": y}

    def logits(owners):
        chunks = [(name, s) for name in owners for s in range(2)]
        ms = [rows_of(place[name] + 4 * cores[s]) for name, s in chunks]
        lhs = jnp.concatenate([hp[m] for m in ms], axis=0)
        parts = [dot(lhs, w_v[a], 1, 0) for a in range(2)]
        top = jnp.maximum(*[jnp.max(jnp.abs(p), axis=1, keepdims=True) for p in parts])
        step = jnp.maximum(top, 1e-30) * (1.0 / 32767.0)
        for n, m in enumerate(ms):
            here = slice(ROWS * n, ROWS * n + ROWS)
            for a in range(2):
                acc[a, m] = parts[a][here]
            own[chunks[n]] = step[here]
        for name in owners:
            sc[6, pl.ds(place[name], 1)] = to_row([own[name, s] for s in range(2)], cores)

    def send_coded(kind):
        for s in range(2):
            for a in range(2):
                near, far = ((R, L), (L, R))[a]
                name = ("O", "LR"[a])[kind]
                code = coded(acc[a, rows_of(place[name] + 4 * cores[s])], own[name, s])
                if kind == 0:
                    qf[a, s] = code
                    start(qf.at[a, s], fbuf.at[s, a], a_send.at[0], a_recv.at[s], yid(c, near))
                else:
                    qd[a, s] = code
                    start(qd.at[a, s], rx.at[s, 0, a], a_send.at[1], a_recv.at[2 + s], yid(cores[s], far))

    logits("O")
    pl.semaphore_wait(barrier, len(peers))
    sce[2] = jnp.broadcast_to(to_row([own["O", s] for s in range(2)], cores), (8, 128))
    for a in range(2):
        start(sce.at[2], sce.at[a], sc_send.at[1], sc_recv.at[0], yid(c, (R, L)[a]))
    send_coded(0)
    logits("RLy")
    for j, yy in enumerate((R, L, O)):
        for s in range(2):
            start(sc.at[6], sc.at[3 * s + j], sc_send.at[0], sc_recv.at[1], yid(cores[s], yy))
    send_coded(1)
    for a in range(2):
        start(acc.at[a, rows_of(y + 4 * pc)], pr.at[a], a_send.at[3], a_recv.at[4], yid(pc, y))

    for a in range(2):
        wt_v[a] = w_v[a].T

    wait_in(sce.at[pl.ds(0, 2)], sc_recv.at[0])
    for s in range(2):
        wait_in(fbuf.at[s], a_recv.at[s])
        for a in range(2):
            near = (R, L)[a]
            by = to_col(sce[a, 0:1], cores[s])
            value = acc[a, rows_of(near + 4 * cores[s])] + decoded(fbuf[s, a]) * by
            cbuf[a, s] = coded(value, by + own["RL"[a], s])
            start(cbuf.at[a, s], rx.at[s, 1, a], a_send.at[2], a_recv.at[2 + s], yid(cores[s], near))

    ht_v[...] = hp[...].T
    loads[3].wait()
    t0 = iota((ROWS, 384), 0)
    token = mine * 24 + t0 + jnp.where(t0 >= 24, 168, 0)
    id_col = jnp.sum(jnp.where(iota((ROWS, 384), 1) == token, id_v[...][None, :], 0), axis=1, keepdims=True)
    id_col = id_col - v * (2 * HALF)
    r, t = iota((96, 96), 0), iota((96, 96), 1)
    w = r - by24(r) * 24
    perm[...] = jnp.where(t == by6(w) * 24 + by24(r) * 6 + w - by6(w) * 6, 1.0, 0.0).astype(BF16)
    r, t = iota((64, ROWS), 0), iota((64, ROWS), 1)
    inner = r & 7
    spread[...] = jnp.where((t == ((r >> 3) & 1) * 24 + (r >> 4) * 6 + inner) & (inner < 6), 1.0, 0.0).astype(BF16)

    r, t = iota((64, ROWS), 0), iota((64, ROWS), 1)
    w = r & 15
    perm1[...] = jnp.where((t == by6(w) * 24 + (r >> 4) * 6 + w - by6(w) * 6) & (w < 12), 1.0, 0.0).astype(BF16)
    r, t = iota((32, 32), 0), iota((32, 32), 1)
    inner = r & 7
    spread1[...] = jnp.where((t == ((r >> 3) & 1) * 16 + (r >> 4) * 6 + inner) & (inner < 6), 1.0, 0.0).astype(BF16)

    wait_in(pr, a_recv.at[4])
    wait_in(sc.at[pl.ds(0, 6)], sc_recv.at[1])
    cols = iota((ROWS, HALF), 1)
    stats = []
    for s in range(2):
        steps = [step_of(3 * s + j, y, c) for j in range(3)]
        wait_in(rx.at[s], a_recv.at[2 + s])
        for a in range(2):
            base = acc[a, rows_of(mine)] if s == 0 else pr[a]
            lg[s, a] = base + decoded(rx[s, 0, a]) * steps[1 - a] + decoded(rx[s, 1, a]) * (steps[a] + steps[2])
        peak = jnp.maximum(*[jnp.max(lg[s, a], axis=1, keepdims=True) for a in range(2)])
        tot = [0.0] * 3
        for a in range(2):
            l = lg[s, a]
            e = jnp.exp((l - peak) * 0.5)
            ev[s, a] = e
            hit = cols == id_col - a * HALF
            for n, term in enumerate((e * e, e, jnp.where(hit, l, 0.0))):
                tot[n] = tot[n] + jnp.sum(term, axis=1, keepdims=True)
        stats.append([peak] + tot)
    for s in range(2):
        stats[s].append(sum(
            jnp.sum(ev[s, a] * (0.5 * (lg[s, a] - lg[1 - s, a])), axis=1, keepdims=True) for a in range(2)
        ))
    xst[0] = jnp.concatenate([to_row([stats[s][n] for s in range(2)]) for n in range(5)] + [jnp.zeros((3, 128), F32)], axis=0)
    for d in range(1, NX):
        start(xst.at[0], xst.at[d], st_sem.at[0], st_sem.at[1], xid(d))
    wait_in(xst.at[pl.ds(1, NX - 1)], st_sem.at[1])

    def merge(parts):
        tops = functools.reduce(jnp.maximum, [p[0:1] for p in parts])
        fs = [jnp.exp((p[0:1] - tops) * 0.5) for p in parts]
        return tops, fs, [sum(p[n:n + 1] * f for p, f in zip(parts, ws)) for n, ws in ((1, [f * f for f in fs]), (2, fs))]

    parts = [xst[d] for d in range(NX)]
    tops, fs, (norm, tau) = merge(parts)
    zst[0] = jnp.concatenate([tops, norm, tau, jnp.zeros((1, 128), F32)], axis=0)
    for d in range(1, NZ):
        start(zst.at[0], zst.at[d], zst_sem.at[0], zst_sem.at[1], zid((z + d) % NZ))
    picked = sum(p[3:4] for p in parts)
    apart = sum(p[4:5] * f for p, f in zip(parts, fs))
    zls[0] = jnp.concatenate([picked, apart, jnp.zeros((2, 128), F32)], axis=0)
    for d in range(1, NZ):
        start(zls.at[0], zls.at[d], zls_sem.at[0], zls_sem.at[1], zid((z + d) % NZ))
    wait_in(zst.at[pl.ds(1, NZ - 1)], zst_sem.at[1])
    tops, fs, (norm, tau) = merge([zst[d] for d in range(NZ)])
    log_total = tops + jnp.log(norm)
    tau_total = tops * 0.5 + jnp.log(tau)

    mr = rows_of(mine)
    log_col = [to_col(log_total, s) for s in range(2)]
    tau_col = [to_col(tau_total, s) for s in range(2)]

    def send_grad(s, a, side):
        src = sg.at[a, mr] if s == 0 else s1.at[a]
        start(src, sg.at[a, mr], g_send.at[1 - s], g_recv.at[2 * side + s], yid(cores[s], ((R, L), (L, R))[side][a]))

    for a in range(2):
        hit = jnp.where(cols == id_col - a * HALF, 1.0, 0.0)
        l = [lg[0, a], lg[1, a]]
        q = [jnp.exp(l[s] * 0.5 - tau_col[s]) for s in range(2)]
        for s in range(2):
            g = (jnp.exp(l[s] - log_col[s]) - hit + (q[s] - q[1 - s])).astype(BF16)
            if s == 0:
                sg[a, mr] = g
            else:
                s1[a] = g
        send_grad(0, a, 0)
    for a in range(2):
        start(s1.at[a], sg.at[a, mr], g_send.at[0], g_recv.at[4], yid(pc, y))
        send_grad(0, a, 1)

    steps = [(mine, y + 4 * pc)] + [(L + 4 * cores[s], R + 4 * cores[s]) for s in range(2)]
    steps += [(O + 4 * cores[s],) for s in range(2)]

    def buffers(k):
        return (hgs, xr, zs, perm, spread, k, ROWS) if k < PAIRS else (hgt, xrt, zst2, perm1, spread1, k - PAIRS, 32)

    def hidden_part(k):
        hg, xb, _, order, _, n, rows = buffers(k)
        part = sum(
            dot(jnp.concatenate([sg[a, rows_of(m)] for m in steps[k]], axis=0), wt_v[a], 1, 0) for a in range(2)
        )
        part = dot(order[...], part.astype(BF16), 1, 0)
        for q in range(NX):
            p = part[rows // 2 * q:rows // 2 * q + rows // 2]
            hg[n, q] = jnp.concatenate([p[:, :384], p[:, 384:]], axis=0).astype(BF16)
        for d in (2, 1, 3):
            start(hg.at[n, (x + d) % NX], xb.at[n, d], x_send.at[k // PAIRS], x_recv.at[k], xid(d))

    def x_sum(k):
        hg, xb, zb, _, order, n, rows = buffers(k)
        wait_in(xb.at[n, pl.ds(1, NX - 1)], x_recv.at[k])
        total = hg[n, x].astype(F32)
        for d in range(1, NX):
            total = total + xb[n, d].astype(F32)
        zb[n] = dot(order[...], total.astype(BF16), 1, 0).astype(BF16)
        for g in range(2 * len(steps[k])):
            zz = steps[k][g // 2] + 8 * (g % 2)
            d = (zz - z + NZ) % NZ

            @pl.when(d != 0)
            def _():
                start(zb.at[n, pl.ds(16 * g, 16)], zr.at[d], z_sem.at[0], z_sem.at[1], zid(zz))

            @pl.when(d == 0)
            def _():
                zr[0] = zb[n, 16 * g:16 * g + 16]

    def two(m):
        return sg.at[:, rows_of(m)]

    def forward(s):
        wait_in(two(L + 4 * cores[s]), g_recv.at[s])
        for a in range(2):
            m = rows_of((L, R)[a] + 4 * cores[s])
            start(sg.at[a, m], sg.at[a, m], g_send.at[0], g_recv.at[5 + s], yid(c, (R, L)[a]))

    wait_in(two(y + 4 * pc), g_recv.at[4])
    hidden_part(0)
    for side in range(2):
        for a in range(2):
            send_grad(1, a, side)
    forward(0)
    wait_in(two(L + 4 * c), g_recv.at[2])
    hidden_part(1)
    forward(1)
    x_sum(0)
    wait_in(two(L + 4 * pc), g_recv.at[3])
    hidden_part(2)
    x_sum(1)

    wait_in(zls.at[pl.ds(1, NZ - 1)], zls_sem.at[1])
    late = [zls[d] for d in range(NZ)]
    picked = sum(p[0:1] for p in late)
    apart = sum(p[1:2] * f for p, f in zip(late, fs))
    ratio = pltpu.roll(apart / tau - tau_total, 64, 1) + tau_total
    loss = log_total - picked + 2.0 * ratio
    lb[0] = jnp.concatenate([loss, jnp.zeros((7, 128), F32)], axis=0)
    for e in range(1, CHUNKS):
        m = (mine + e) % CHUNKS
        start(lb.at[0], lb.at[e], l_sem.at[0], l_sem.at[1], yid(m // 4, m % 4))
    for s in range(2):
        wait_in(two(O + 4 * cores[s]), g_recv.at[5 + s])
        hidden_part(3 + s)
    x_sum(2)
    for a in range(2):
        wg_out[0, :, a * HALF:(a + 1) * HALF] = dot(ht_v[...], sg[a], 1, 0).astype(BF16)
        x_sum(3 + a)

    wait_in(lb.at[pl.ds(1, CHUNKS - 1)], l_sem.at[1])
    lanes = iota((1, 128), 1)
    mixed = jnp.zeros((1, 128), F32)
    for i in range(4):
        m = (4 * y + i) % CHUNKS
        row = lb[(mine - m + CHUNKS) % CHUNKS, 0:1]
        row = jnp.where(m // 4 == c, row, pltpu.roll(row, 64, 1))
        row = jnp.where(y // 2 == 0, row, pltpu.roll(row, 104, 1))
        if i:
            row = pltpu.roll(row, 24 * i, 1)
        mixed = jnp.where((lanes >= 24 * i) & (lanes < 24 * i + 24), row, mixed)
    loss_out[...] = mixed[:, :96]

    wait_in(zr.at[pl.ds(1, NZ - 1)], z_sem.at[1])
    total = sum(zr[d].astype(F32) for d in range(NZ))
    hg_out[0] = jnp.concatenate([total[:8], total[8:]], axis=1)[:6].astype(BF16)

    wait_out(qf, a_send.at[0])
    wait_out(qd, a_send.at[1])
    wait_out(cbuf, a_send.at[2])
    wait_out(pr, a_send.at[3])
    wait_out(sc.at[pl.ds(0, 6)], sc_send.at[0])
    wait_out(sce.at[pl.ds(0, 2)], sc_send.at[1])
    wait_out(xst.at[pl.ds(1, NX - 1)], st_sem.at[0])
    wait_out(zst.at[pl.ds(1, NZ - 1)], zst_sem.at[0])
    wait_out(zls.at[pl.ds(1, NZ - 1)], zls_sem.at[0])
    wait_out(lb.at[pl.ds(1, CHUNKS - 1)], l_sem.at[0])
    wait_out(sg.at[:, pl.ds(0, 5 * ROWS)], g_send.at[0])
    wait_out(sg.at[:, pl.ds(0, 2 * ROWS)], g_send.at[1])
    wait_out(xr.at[:, pl.ds(1, NX - 1)], x_send.at[0])
    wait_out(xrt.at[:, pl.ds(1, NX - 1)], x_send.at[1])
    wait_out(zr.at[pl.ds(1, NZ - 1)], z_sem.at[0])


def finish(*refs):
    copies = [pltpu.make_async_copy(refs[i], refs[3 + i], refs[6].at[i]) for i in range(3)]
    for cp in copies:
        cp.start()
    for cp in copies:
        cp.wait()


def body(hidden, head_weight, token_ids):
    dma = pltpu.SemaphoreType.DMA
    outs = pl.pallas_call(
        kernel,
        out_shape=(
            pltpu.VMEM((1, 96), F32),
            pltpu.VMEM((1, 768, 2 * HALF), BF16),
            pltpu.VMEM((1, 6, 768), BF16),
        ),
        in_specs=[pl.BlockSpec(memory_space=pl.ANY)] * 3,
        out_specs=(pl.BlockSpec(memory_space=pltpu.VMEM),) * 3,
        scratch_shapes=[
            pltpu.VMEM((384,), I32),
            pltpu.VMEM((2, 768, HALF), BF16),
            pltpu.VMEM((2, HALF, 768), BF16),
            pltpu.VMEM((384, 768), BF16),
            pltpu.VMEM((384, 768), BF16),
            pltpu.VMEM((768, 384), BF16),
            pltpu.VMEM((2, 384, HALF), F32),
            pltpu.VMEM((2, 2, ROWS, HALF), I16),
            pltpu.VMEM((2, 2, ROWS, HALF), I16),
            pltpu.VMEM((2, 2, ROWS, HALF), I16),
            pltpu.VMEM((2, 2, ROWS, HALF), I16),
            pltpu.VMEM((2, 2, 2, ROWS, HALF), I16),
            pltpu.VMEM((2, ROWS, HALF), F32),
            pltpu.VMEM((2, 2, ROWS, HALF), F32),
            pltpu.VMEM((2, 384, HALF), BF16),
            pltpu.VMEM((2, ROWS, HALF), BF16),
            pltpu.VMEM((PAIRS, NX, ROWS, 384), BF16),
            pltpu.VMEM((PAIRS, NX, ROWS, 384), BF16),
            pltpu.VMEM((PAIRS, 64, 384), BF16),
            pltpu.VMEM((NZ, 16, 384), BF16),
            pltpu.VMEM((2, NX, 32, 384), BF16),
            pltpu.VMEM((2, NX, 32, 384), BF16),
            pltpu.VMEM((2, 32, 384), BF16),
            pltpu.VMEM((7, 8, 128), F32),
            pltpu.VMEM((3, 8, 128), F32),
            pltpu.VMEM((NX, 8, 128), F32),
            pltpu.VMEM((NZ, 4, 128), F32),
            pltpu.VMEM((NZ, 4, 128), F32),
            pltpu.VMEM((CHUNKS, 8, 128), F32),
            pltpu.VMEM((96, 96), BF16),
            pltpu.VMEM((64, ROWS), BF16),
            pltpu.VMEM((64, ROWS), BF16),
            pltpu.VMEM((32, 32), BF16),
            pltpu.VMEM((2, 2, ROWS, HALF), F32),
            dma((4,)),
            dma((4,)), dma((5,)),
            dma((2,)), dma((2,)),
            dma((2,)), dma((2,)), dma((2,)), dma((2,)),
            dma((2,)), dma((7,)),
            dma((2,)), dma((PAIRS + 2,)),
            dma((2,)),
        ],
        compiler_params=pltpu.CompilerParams(
            collective_id=0, has_side_effects=True, vmem_limit_bytes=60 * 1024 * 1024
        ),
        cost_estimate=pl.CostEstimate(flops=2400000000, bytes_accessed=5000000, transcendentals=400000),
    )(hidden, head_weight, token_ids)
    return pl.pallas_call(
        finish,
        out_shape=tuple(jax.ShapeDtypeStruct(o.shape, o.dtype) for o in outs),
        in_specs=[pl.BlockSpec(memory_space=pltpu.VMEM)] * 3,
        out_specs=(pl.BlockSpec(memory_space=pl.ANY),) * 3,
        scratch_shapes=[dma((3,))],
        compiler_params=pltpu.CompilerParams(vmem_limit_bytes=1024 * 1024),
    )(*outs)


def solution(mesh):
    return jax.shard_map(
        body,
        mesh=mesh,
        in_specs=(P("rep", None, "tok"), P("rep", "tok", "vocab"), P()),
        out_specs=(P("rep", "tok"), P("rep", "tok", "vocab"), P("rep", "vocab", "tok")),
        check_vma=False,
    )
```
